256 devices in a mesh: seq: 32 (over z, y_lo, core), qry: 8 (over x, y_hi).
Axes of the slice: x: 4, y: 4 (y_hi: 2, y_lo: 2; y = y_hi * 2 + y_lo), z: 8, core: 2. Of those that a mesh axis runs over, the one named last changes fastest.
Arguments:
- x_inner: bfloat16 [8, 32768, 2048], P('qry', 'seq'), may hold values from -6 to 6
- z_gate: bfloat16 [8, 32768, 2048], P('qry', 'seq'), may hold values from -6 to 6
- b_proj: bfloat16 [8, 32768, 128], P('qry', 'seq'), may hold values from -0.5 to 0.5
- c_proj: bfloat16 [8, 32768, 128], P('qry', 'seq'), may hold values from -0.5 to 0.5
- decays: float32 [8, 32, 32768], P('qry', None, 'seq'), may hold values from 0 to 1
- d_skip: float32 [32], replicated, may hold values from 0.5 to 2
- norm_gain: float32 [2048], replicated, may hold values from 0.1 to 1.9
- w_head: bfloat16 [2048, 128], replicated, may hold values from -0.125 to 0.125
- queries: bfloat16 [128, 32, 128], P('qry'), may hold values from -6 to 6
- valid_len: int32 [8, 256], P('qry', 'seq'), may hold values from 32 to 128, as said below
- pair_ids: int32 [128], replicated, may hold values from 0 to 2047
Outputs:
- maxsim_scores: float32 [8, 256, 128], P('qry', 'seq')
- paired_score: float32 [128], replicated
The draws below stay inside these ranges and needn't reach their ends.
Inputs may be any that keep to these rules, and one draw needn't show every extreme that they name: `valid_len`: in every document at least one passage has all 128 tokens valid. `pair_ids`: passage index d * 256 + k.
All inputs are finite; a program needn't handle non-finite values.
Results may differ from the reference program's by a relative error of at most 0.002.
Values may be sent and summed in bfloat16 or wider, within the bound.
No kernel may reach another device: no remote copies, remote signals or barrier semaphores. Data moves between devices by JAX's collectives and lax.ppermute only.
A program may use at most 192 MiB of HBM per device.

```python
import math
import jax
import jax.numpy as jnp
from jax import lax

STATE_HEADS = 32
HEAD_DIM = 64
STATE = 128
EMB = 128
QTOK = 32
PLEN = 128
SPAN = 128
TOK_DEV = 1024
INNER = 2048
DOCUMENT_TOKENS = 32768
DOCUMENT_COUNT = 8
NPD = 256
QTOT = 128


def draw_decays(key, part):
    key = jax.random.fold_in(key, 5)
    key_rows = jax.random.split(key, 8)
    slow_share = 0.35
    switch_share = 0.35
    head_roll = jax.random.uniform(key_rows[0], (DOCUMENT_COUNT, STATE_HEADS, 1))
    slow_heads = head_roll < slow_share
    switch_heads = (head_roll >= slow_share) & (head_roll < slow_share + switch_share)
    fast_rate = 1.0 / jax.random.uniform(key_rows[1], (DOCUMENT_COUNT, STATE_HEADS, 1), minval=30.0, maxval=50.0)
    slow_rate = math.log(10.0) * jax.random.uniform(key_rows[2], (DOCUMENT_COUNT, STATE_HEADS, 1), minval=0.05, maxval=0.2) / DOCUMENT_TOKENS
    shard_count = DOCUMENT_TOKENS // TOK_DEV
    switch_shard = jax.random.randint(key_rows[7], (DOCUMENT_COUNT, STATE_HEADS, 1), 2, max(shard_count, 3))
    token_positions = jnp.arange(DOCUMENT_TOKENS, dtype=jnp.int32)
    before_switch = token_positions[None, None, :] < switch_shard * TOK_DEV
    keeps_slow = slow_heads | switch_heads & before_switch
    decay_speed = jnp.where(keeps_slow, slow_rate, fast_rate)
    blocks = DOCUMENT_TOKENS // SPAN
    block_multiplier = jnp.exp(jax.random.uniform(key_rows[3], (DOCUMENT_COUNT, STATE_HEADS, blocks, 1), minval=-math.log(2.0), maxval=math.log(2.0)))
    block_multiplier = jnp.broadcast_to(block_multiplier, (DOCUMENT_COUNT, STATE_HEADS, blocks, SPAN)).reshape(DOCUMENT_COUNT, STATE_HEADS, DOCUMENT_TOKENS)
    jaggedness = jax.random.uniform(key_rows[4], (DOCUMENT_COUNT, STATE_HEADS, DOCUMENT_TOKENS), minval=0.5, maxval=1.5)
    marked_places = jax.random.randint(key_rows[5], (DOCUMENT_COUNT, 1, 1, 2), 0, DOCUMENT_TOKENS)
    spike_match = jnp.any(token_positions[None, None, :, None] == marked_places, axis=-1)
    spike_penalty = jax.random.uniform(key_rows[6], (DOCUMENT_COUNT, STATE_HEADS, DOCUMENT_TOKENS), minval=math.log(0.65), maxval=math.log(0.8))
    decay_logarithm = -decay_speed * block_multiplier * jaggedness + jnp.where(spike_match, spike_penalty, 0.0)
    return jnp.exp(decay_logarithm).astype(jnp.float32)


def draw_valid_len(key, part):
    key = jax.random.fold_in(key, 7)
    key_rows = jax.random.split(key, 2)
    counts = jax.random.randint(key_rows[0], (DOCUMENT_COUNT, NPD), max(1, PLEN // 4), PLEN + 1)
    full_slot = jax.random.randint(key_rows[1], (DOCUMENT_COUNT, 1), 0, NPD)
    slot_index = jnp.arange(NPD, dtype=jnp.int32)[None, :]
    return jnp.where(slot_index == full_slot, PLEN, counts).astype(jnp.int32)


def set_ends(drawn, rng, low, top_value):
    place = [jax.random.randint(jax.random.fold_in(rng, axis), (), 0, length) for axis, length in enumerate(drawn.shape)]
    longest = drawn.shape.index(max(drawn.shape))
    next_to = place[:longest] + [(place[longest] + 1) % drawn.shape[longest]] + place[longest + 1:]
    return drawn.at[tuple(place)].set(low).at[tuple(next_to)].set(top_value)


def block_scale(own_key, extent, shards, low, largest):
    loudness = 1.0
    for dim, shards_of in shards:
        draws = jax.random.uniform(jax.random.fold_in(jax.random.fold_in(own_key, 6), dim), (shards_of,), jnp.float32, low / len(shards), largest / len(shards))
        loudness = loudness * jnp.repeat(jnp.exp(draws), extent[dim] // shards_of).reshape((-1,) + (1,) * (len(extent) - 1 - dim))
    return loudness


def scatter_about(stream_key, extent, scale, reach, cuts=(), kind=jnp.bfloat16):
    values = jax.random.normal(stream_key, extent, jnp.float32) * scale
    if len(cuts) > 0:
        values = block_scale(stream_key, extent, cuts, -0.22, 0.18) * values
    return jnp.clip(values, min=-reach, max=reach).astype(kind)


def setup_inputs(seed: int = 0) -> dict:
    keys = jax.random.split(jax.random.key(seed), 12)
    return {
        "x_inner": scatter_about(keys[0], (DOCUMENT_COUNT, DOCUMENT_TOKENS, INNER), 1.0, 6.0, ((0, 8), (1, 32))),
        "z_gate": scatter_about(keys[1], (DOCUMENT_COUNT, DOCUMENT_TOKENS, INNER), 1.0, 6.0, ((0, 8), (1, 32))),
        "b_proj": scatter_about(keys[2], (DOCUMENT_COUNT, DOCUMENT_TOKENS, STATE), STATE ** -0.5, 0.5, ((0, 8), (1, 32))),
        "c_proj": scatter_about(keys[3], (DOCUMENT_COUNT, DOCUMENT_TOKENS, STATE), STATE ** -0.5, 0.5, ((0, 8), (1, 32))),
        "decays": draw_decays(jax.random.fold_in(keys[11], 71), 0),
        "d_skip": jnp.clip(jax.random.uniform(keys[5], (STATE_HEADS,), jnp.float32, 0.5, 2.0), 0.5, 2.0),
        "norm_gain": jnp.clip(1.0 + 0.18 * jax.random.normal(keys[6], (INNER,), jnp.float32), 0.1, 1.9),
        "w_head": scatter_about(keys[7], (INNER, EMB), INNER ** -0.5, 0.125),
        "queries": scatter_about(keys[8], (QTOT, QTOK, EMB), 1.0, 6.0, ((0, 8),)),
        "valid_len": draw_valid_len(jax.random.fold_in(keys[11], 71), 0),
        "pair_ids": set_ends(jax.random.randint(keys[10], (QTOT,), 0, DOCUMENT_COUNT * NPD), jax.random.fold_in(keys[10], 1), 0, (DOCUMENT_COUNT * NPD) - 1).astype(jnp.int32),
    }


def encode_document(x_doc, z_doc, b_doc, c_doc, decay_doc, d_skip, norm_gain, w_head):
    spans = x_doc.shape[0] // SPAN
    x_all = x_doc.reshape(spans, SPAN, STATE_HEADS, HEAD_DIM)
    z_all = z_doc.reshape(spans, SPAN, STATE_HEADS * HEAD_DIM)
    b_all = b_doc.reshape(spans, SPAN, STATE)
    c_all = c_doc.reshape(spans, SPAN, STATE)
    log_all = jnp.log(decay_doc).reshape(STATE_HEADS, spans, SPAN).transpose(1, 0, 2)
    causal = jnp.tril(jnp.ones((SPAN, SPAN), dtype=bool))

    def span_step(carried, inputs):
        x_span, z_span, b_span, c_span, log_span = inputs
        cumulative = jnp.cumsum(log_span, axis=-1)
        cross_cb = jnp.dot(c_span, b_span.T, preferred_element_type=jnp.float32)
        spread = cumulative[:, :, None] - cumulative[:, None, :]
        mixing = (cross_cb[None] * jnp.exp(jnp.where(causal[None], spread, -jnp.inf))).astype(jnp.bfloat16)
        x_wide = x_span.astype(jnp.float32)
        y_out = jnp.einsum('hts,shp->thp', mixing.astype(jnp.float32), x_wide)
        read_out = jnp.einsum('tn,hpn->thp', c_span.astype(jnp.float32), carried, precision=lax.Precision.HIGHEST)
        y_out = y_out + jnp.exp(cumulative).T[:, :, None] * read_out
        y_out = y_out + d_skip[None, :, None] * x_wide
        weights = jnp.exp(cumulative[:, -1:] - cumulative)
        weighted_b = (b_span.astype(jnp.float32)[None] * weights[:, :, None]).astype(jnp.bfloat16)
        fresh_state = jnp.einsum('hsn,shp->hpn', weighted_b.astype(jnp.float32), x_wide)
        carried = jnp.exp(cumulative[:, -1])[:, None, None] * carried + fresh_state
        gated = y_out.reshape(SPAN, STATE_HEADS * HEAD_DIM) * jax.nn.silu(z_span.astype(jnp.float32))
        grouped = gated.reshape(SPAN, STATE_HEADS, HEAD_DIM)
        scaled = grouped * lax.rsqrt(lax.optimization_barrier(jnp.mean(grouped * grouped, axis=-1, keepdims=True)) + 1e-05)
        normed = (scaled.reshape(SPAN, STATE_HEADS * HEAD_DIM) * norm_gain).astype(jnp.bfloat16)
        embedded = jnp.dot(normed, w_head, preferred_element_type=jnp.float32)
        embedded = embedded * lax.rsqrt(lax.optimization_barrier(jnp.sum(embedded * embedded, axis=-1, keepdims=True)) + 1e-06)
        return (carried, embedded.astype(jnp.bfloat16))
    zero_state = jnp.zeros((STATE_HEADS, HEAD_DIM, STATE), jnp.float32)
    unused_state, vectors = lax.scan(span_step, zero_state, (x_all, z_all, b_all, c_all, log_all))
    return vectors.reshape(spans * SPAN, EMB)

def reference(x_inner, z_gate, b_proj, c_proj, decays, d_skip, norm_gain, w_head, queries, valid_len, pair_ids):
    query_wide = queries.astype(jnp.float32)
    query_vecs = (query_wide * lax.rsqrt(lax.optimization_barrier(jnp.sum(query_wide * query_wide, axis=-1, keepdims=True)) + 1e-06)).astype(jnp.bfloat16)
    flat_queries = query_vecs.reshape(QTOT * QTOK, EMB)
    slot_index = jnp.arange(PLEN, dtype=jnp.int32)
    doc_scores = []
    for doc_index in range(DOCUMENT_COUNT):
        vectors = encode_document(x_inner[doc_index], z_gate[doc_index], b_proj[doc_index], c_proj[doc_index], decays[doc_index], d_skip, norm_gain, w_head)
        passage_vecs = vectors.reshape(NPD, PLEN, EMB)
        token_mask = slot_index[None, :] < valid_len[doc_index][:, None]

        def score_passage(inputs):
            passage, mask_row = inputs
            tile_sims = jnp.dot(passage, flat_queries.T, preferred_element_type=jnp.float32)
            tile_sims = jnp.where(mask_row[:, None], tile_sims, -2.0)
            return lax.optimization_barrier(jnp.sum(lax.optimization_barrier(jnp.max(tile_sims, axis=0)).reshape(QTOT, QTOK), axis=-1))
        doc_scores.append(lax.map(score_passage, (passage_vecs, token_mask)))
    maxsim_scores = jnp.stack(doc_scores)
    flat_scores = maxsim_scores.reshape(DOCUMENT_COUNT * NPD, QTOT)
    paired_score = jnp.take_along_axis(flat_scores, pair_ids[None, :].astype(jnp.int32), axis=0)[0]
    return (maxsim_scores, paired_score)
```

```python
import functools

import jax
import jax.numpy as jnp
from jax import lax
from jax.experimental import pallas as pl
from jax.experimental.pallas import tpu as pltpu
from jax.sharding import Mesh
from jax.sharding import PartitionSpec as P

HEADS = 32
HEAD_DIM = 64
STATE = 128
SPAN = 128
TOKENS = 1024
SPANS = TOKENS // SPAN
INNER = HEADS * HEAD_DIM
PAIRS = HEADS // 2
WIDE = 512
CHUNKS = INNER // WIDE
HALF = STATE // 2
ROWS = HALF + 16
QTOK = 32
QTOT = 128
EMB = 128
BLOCK = 256
F32 = jnp.float32
BF16 = jnp.bfloat16
NT = (((1,), (1,)), ((), ()))


def dot(a, b):
    return jnp.dot(a, b, preferred_element_type=F32)


def dot_nt(a, b):
    return lax.dot_general(a, b, NT, preferred_element_type=F32)


def iota(shape, dim):
    return lax.broadcasted_iota(jnp.int32, shape, dim)


def ones_where(cond):
    return jnp.where(cond, 1.0, 0.0).astype(BF16)


def split2(v):
    high = v.astype(BF16)
    return high, (v - high.astype(F32)).astype(BF16)


def split3(v):
    high = v.astype(BF16)
    rest = v - high.astype(F32)
    mid = rest.astype(BF16)
    return high, mid, (rest - mid.astype(F32)).astype(BF16)


def head_selector(rows, first_head, columns):
    head = iota((rows, columns), 0) & (HEADS - 1)
    return ones_where(head == first_head + (iota((rows, columns), 1) >> 6))


def states_kernel(core_ref, dec_ref, b_ref, x_ref, keep_ref, send_ref, w_ref, bt_ref, d_ref):
    step = pl.program_id(0)

    @pl.when(step == 0)
    def _():
        row, col = iota((SPAN + 16, SPAN), 0), iota((SPAN + 16, SPAN), 1)
        after = ones_where((col > row) | (row >= SPAN))
        after = jnp.concatenate([after, after, after], axis=1)
        later = jnp.zeros((16, HEADS), F32)
        for c in reversed(range(SPANS)):
            rows = slice(c * SPAN, (c + 1) * SPAN)
            logs = jnp.concatenate(split3(jnp.log2(dec_ref[:, rows])), axis=1)
            sums = dot_nt(after, logs)
            high, low = split2(jnp.exp2(sums[:SPAN] + later[:1]))
            w_ref[rows, :] = jnp.concatenate([high, low], axis=1)
            later = later + sums[SPAN:]
            bt_ref[:, rows] = b_ref[rows, :].T
        high, low = split2(jnp.exp2(later))
        place = iota((16, HEADS), 0)
        zero = jnp.zeros((16, HEADS), F32)
        d_ref[...] = jnp.where(
            place == 0, high.astype(F32), jnp.where(place == 1, low.astype(F32), zero)
        ).astype(BF16)

    selector = head_selector(2 * HEADS, step * (WIDE // HEAD_DIM), WIDE)
    weighted = (x_ref[...].astype(F32) * dot(w_ref[...], selector)).astype(BF16)
    state = dot(bt_ref[...], weighted)
    decay = dot(d_ref[...], selector[:HEADS]).astype(BF16)
    lower = core_ref[0] == 0
    mine = jnp.where(lower, state[:HALF], state[HALF:]).astype(BF16)
    other = jnp.where(lower, state[HALF:], state[:HALF]).astype(BF16)
    for k in range(WIDE // 128):
        lanes = slice(k * 128, (k + 1) * 128)
        keep_ref[k, :HALF, :] = mine[:, lanes]
        keep_ref[k, HALF:, :] = decay[:, lanes]
        send_ref[k, :HALF, :] = other[:, lanes]
        send_ref[k, HALF:, :] = decay[:, lanes]


def local_kernel(
    dec_ref, b_ref, c_ref, x_ref, z_ref, skip_ref, y_ref, gate_ref, g_ref, carry_ref, prior_ref, e_ref
):
    step = pl.program_id(0)

    @pl.when(step == 0)
    def _():
        carry_ref[...] = jnp.zeros_like(carry_ref)
        prior_ref[...] = jnp.zeros_like(prior_ref)
        e_ref[...] = head_selector(2 * HEADS, 0, INNER)

    row, col = iota((SPAN, SPAN), 0), iota((SPAN, SPAN), 1)
    until = ones_where(col <= row)
    after = ones_where(col > row)
    sums_of = jnp.concatenate([until, after, jnp.ones((16, SPAN), BF16)], axis=0)
    sums_of = jnp.concatenate([sums_of, sums_of, sums_of], axis=1)
    logs = jnp.concatenate(split3(jnp.log2(dec_ref[...])), axis=1)
    sums = dot_nt(sums_of, logs)
    cum = sums[:SPAN]
    rows_until = ones_where(row <= col)
    cum_rows = dot(logs, jnp.concatenate([rows_until, rows_until, rows_until], axis=0))
    prior = prior_ref[...]
    prior_ref[...] = prior + sums[2 * SPAN : 2 * SPAN + 8]
    high, low = split2(jnp.exp2(cum + prior[:1]))
    g_ref[...] = jnp.concatenate([high, low], axis=1)
    factors = jnp.concatenate(split2(jnp.exp2(sums)), axis=1)
    c_span, b_span = c_ref[...], b_ref[...]
    b_turned = b_span.T
    cross = jnp.where(col <= row, dot_nt(c_span, b_span), 0.0)
    left = col < HEAD_DIM
    for j in range(CHUNKS):
        wide = slice(j * WIDE, (j + 1) * WIDE)
        spread_out = dot(factors, e_ref[:, wide])
        carry = carry_ref[:, wide]
        read = dot(c_span, carry.astype(BF16)) * spread_out[:SPAN]
        x_wide = x_ref[:, wide].astype(F32)
        parts = []
        for k in range(WIDE // 128):
            mixes = []
            for h in (j * 8 + 2 * k, j * 8 + 2 * k + 1):
                spread = jnp.minimum(cum[:, h : h + 1] - cum_rows[h : h + 1, :], 0.0)
                mixes.append((jnp.exp2(spread) * cross).astype(BF16))
            x_pair = x_ref[:, j * WIDE + k * 128 : j * WIDE + (k + 1) * 128]
            none = jnp.zeros_like(x_pair)
            x_both = jnp.concatenate(
                [jnp.where(left, x_pair, none), jnp.where(left, none, x_pair)], axis=0
            )
            parts.append(dot(jnp.concatenate(mixes, axis=1), x_both))
        y = jnp.concatenate(parts, axis=1) + read + skip_ref[:, wide] * x_wide
        y_ref[:, wide] = y.astype(BF16)
        weighted = (x_wide * spread_out[SPAN : 2 * SPAN]).astype(BF16)
        carry_ref[:, wide] = spread_out[2 * SPAN : 2 * SPAN + 1] * carry + dot(b_turned, weighted)
        z_half = 0.5 * z_ref[:, wide].astype(F32)
        gate_ref[:, wide] = (z_half + z_half * jnp.tanh(z_half)).astype(BF16)


def scan_kernel(in_ref, out_ref):
    carry = jnp.zeros((HALF, 128), F32)
    for k in range(PAIRS):
        out_ref[k] = carry.astype(BF16)
        decay = in_ref[k, HALF : HALF + 8, :].astype(F32)
        decay = decay[0:1] + decay[1:2]
        carry = decay * carry + in_ref[k, :HALF, :].astype(F32)


def score_kernel(
    base_ref, valid_ref, keep_ref, got_ref, c_ref, g_ref, y_ref, gate_ref, gain_ref, head_ref,
    q_ref, pair_ref, score_ref, paired_ref, e_ref, mean_ref, best_ref
):
    step = pl.program_id(0)

    @pl.when(step == 0)
    def _():
        e_ref[...] = head_selector(2 * HEADS, 0, INNER)
        same = (iota((256, 256), 0) >> 6) == (iota((256, 256), 1) >> 6)
        mean_ref[...] = jnp.where(same, 1.0 / HEAD_DIM, 0.0).astype(BF16)

    factors, c_part = g_ref[...], c_ref[...]
    embedded = jnp.zeros((BLOCK, EMB), F32)
    for j in range(CHUNKS):
        wide = slice(j * WIDE, (j + 1) * WIDE)
        entering = jnp.concatenate(
            [
                jnp.concatenate([keep_ref[4 * j + k], got_ref[4 * j + k]], axis=0)
                for k in range(WIDE // 128)
            ],
            axis=1,
        )
        y = y_ref[:, wide].astype(F32) + dot(factors, e_ref[:, wide]) * dot(c_part, entering)
        gated = y * gate_ref[:, wide].astype(F32)
        squares = (gated * gated).astype(BF16)
        means = jnp.concatenate(
            [dot(squares[:, k : k + 256], mean_ref[...]) for k in range(0, WIDE, 256)], axis=1
        )
        normed = (gated * lax.rsqrt(means + 1e-05) * gain_ref[:, wide]).astype(BF16)
        embedded = embedded + dot(normed, head_ref[wide, :])
    embedded = embedded * lax.rsqrt(jnp.sum(embedded * embedded, axis=1, keepdims=True) + 1e-06)
    for p in range(BLOCK // SPAN):
        passage = step * (BLOCK // SPAN) + p
        vectors = embedded[p * SPAN : (p + 1) * SPAN]
        kept = iota((SPAN, EMB), 0) < valid_ref[0, passage]
        vectors = jnp.where(kept, vectors, vectors[:1]).astype(BF16)
        for j in range(QTOK * QTOT // 1024):
            lanes = slice(j * 1024, (j + 1) * 1024)
            sims = dot_nt(vectors, q_ref[lanes, :])
            best_ref[pl.ds(passage, 1), lanes] = jnp.max(sims, axis=0, keepdims=True)

    @pl.when(step == TOKENS // BLOCK - 1)
    def _():
        total = best_ref[:, :QTOT]
        for i in range(1, QTOK):
            total = total + best_ref[:, i * QTOT : (i + 1) * QTOT]
        score_ref[...] = total
        matched = pair_ref[...] == base_ref[0] + iota((SPANS, QTOT), 0)
        paired = jnp.sum(jnp.where(matched, total, 0.0), axis=0, keepdims=True)
        paired_ref[...] = jnp.broadcast_to(paired, paired_ref.shape)


def whole(shape, space=None):
    kind = {} if space is None else {"memory_space": space}
    return pl.BlockSpec(shape, lambda i: (0,) * len(shape), **kind)


def params(mib):
    return pltpu.CompilerParams(
        dimension_semantics=("arbitrary",), vmem_limit_bytes=mib * 1024 * 1024
    )


def cost(flops, bytes_accessed, transcendentals=0):
    return pl.CostEstimate(
        flops=flops, bytes_accessed=bytes_accessed, transcendentals=transcendentals
    )


def device_states(core, decays, b, x):
    smem = pl.BlockSpec(memory_space=pltpu.SMEM)
    packed = jax.ShapeDtypeStruct((PAIRS, ROWS, 128), BF16)
    blocks = pl.BlockSpec((WIDE // 128, ROWS, 128), lambda i: (i, 0, 0))
    return pl.pallas_call(
        states_kernel,
        grid=(CHUNKS,),
        in_specs=[
            smem,
            whole((HEADS, TOKENS)),
            whole((TOKENS, STATE)),
            pl.BlockSpec((TOKENS, WIDE), lambda i: (0, i)),
        ],
        out_specs=[blocks, blocks],
        out_shape=[packed, packed],
        scratch_shapes=[
            pltpu.VMEM((TOKENS, 2 * HEADS), BF16),
            pltpu.VMEM((STATE, TOKENS), BF16),
            pltpu.VMEM((16, HEADS), BF16),
        ],
        compiler_params=params(20),
        cost_estimate=cost(10**9, 5 * 10**6),
        name="device_states",
    )(core, decays, b, x)


def local_part(decays, b, c, x, z, skip):
    def tokens(width):
        return pl.BlockSpec((SPAN, width), lambda i: (i, 0))

    return pl.pallas_call(
        local_kernel,
        grid=(SPANS,),
        in_specs=[
            pl.BlockSpec((HEADS, SPAN), lambda i: (0, i)),
            tokens(STATE),
            tokens(STATE),
            tokens(INNER),
            tokens(INNER),
            whole((1, INNER)),
        ],
        out_specs=[tokens(INNER), tokens(INNER), tokens(2 * HEADS)],
        out_shape=[
            jax.ShapeDtypeStruct((TOKENS, INNER), BF16),
            jax.ShapeDtypeStruct((TOKENS, INNER), BF16),
            jax.ShapeDtypeStruct((TOKENS, 2 * HEADS), BF16),
        ],
        scratch_shapes=[
            pltpu.VMEM((STATE, INNER), F32),
            pltpu.VMEM((8, HEADS), F32),
            pltpu.VMEM((2 * HEADS, INNER), BF16),
        ],
        compiler_params=params(20),
        cost_estimate=cost(8 * 10**9, 17 * 10**6, 6 * 10**6),
        name="local_part",
    )(decays, b, c, x, z, skip)


def scan_chips(states):
    return pl.pallas_call(
        scan_kernel,
        out_shape=jax.ShapeDtypeStruct((PAIRS, HALF, 128), BF16),
        cost_estimate=cost(10**6, 600_000),
        name="scan_chips",
    )(states)


def scores(base, valid_len, keep, got, c, growth, y, gate, gain, w_head, q, pair_ids):
    def tokens(width):
        return pl.BlockSpec((BLOCK, width), lambda i: (i, 0))

    smem = pl.BlockSpec(memory_space=pltpu.SMEM)
    half = whole((PAIRS, HALF, 128))
    everyone = 256
    return pl.pallas_call(
        score_kernel,
        grid=(TOKENS // BLOCK,),
        in_specs=[
            smem,
            smem,
            half,
            half,
            tokens(STATE),
            tokens(2 * HEADS),
            tokens(INNER),
            tokens(INNER),
            whole((1, INNER)),
            whole((INNER, EMB)),
            whole((QTOK * QTOT, EMB)),
            whole((1, QTOT)),
        ],
        out_specs=[whole((SPANS, QTOT)), whole((everyone, QTOT))],
        out_shape=[
            jax.ShapeDtypeStruct((SPANS, QTOT), F32),
            jax.ShapeDtypeStruct((everyone, QTOT), F32),
        ],
        scratch_shapes=[
            pltpu.VMEM((2 * HEADS, INNER), BF16),
            pltpu.VMEM((256, 256), BF16),
            pltpu.VMEM((SPANS, QTOK * QTOT), F32),
        ],
        compiler_params=params(24),
        cost_estimate=cost(6 * 10**9, 11 * 10**6, 2 * 10**6),
        name="scores",
    )(base, valid_len, keep, got, c, growth, y, gate, gain, w_head, q, pair_ids)


def swap_cores(v):
    return lax.ppermute(v, "core", [(0, 1), (1, 0)])


def decay_of(packed):
    return packed[:, HALF : HALF + 1].astype(F32) + packed[:, HALF + 1 : HALF + 2].astype(F32)


def on_device(
    x_inner, z_gate, b_proj, c_proj, decays, d_skip, norm_gain, w_head, queries, valid_len, pair_ids
):
    core = lax.axis_index("core")
    x, z, b, c, decay = x_inner[0], z_gate[0], b_proj[0], c_proj[0], decays[0]

    wide = queries.astype(F32)
    q = (wide * lax.rsqrt(jnp.sum(wide * wide, axis=-1, keepdims=True) + 1e-06)).astype(BF16)
    q = jnp.broadcast_to(q.transpose(1, 0, 2)[None], (8, QTOK, 16, EMB))
    q = lax.all_to_all(q, ("x", "y_hi"), 0, 0, tiled=True)
    q = q.transpose(1, 0, 2, 3).reshape(QTOK * QTOT, EMB)

    own, send = device_states(core.reshape(1), decay, b, x)
    got = swap_cores(send)
    lower = core == 0
    first = jnp.where(lower, own, got)
    second = jnp.where(lower, got, own)
    d_first, d_second = decay_of(first), decay_of(second)
    chip = d_second * first[:, :HALF].astype(F32) + second[:, :HALF].astype(F32)
    high, low = split2(d_first * d_second)
    fill = jnp.zeros((PAIRS, 14, 128), BF16)
    packed = jnp.concatenate([chip.astype(BF16), high, low, fill], axis=1)
    by_pair = lax.all_to_all(packed, ("z", "y_lo"), 0, 0, tiled=True)

    y_local, gate, growth = local_part(
        decay, b, c, x, z, jnp.repeat(d_skip, HEAD_DIM).reshape(1, INNER)
    )

    entering = lax.all_to_all(scan_chips(by_pair), ("z", "y_lo"), 0, 0, tiled=True)
    after = (
        d_first * entering.astype(F32) + first[:, :HALF].astype(F32)
    ).astype(BF16)
    keep = jnp.where(lower, entering, after)
    got = swap_cores(jnp.where(lower, after, entering))
    c_turned = jnp.where(lower, c, jnp.roll(c, HALF, axis=1))

    document = lax.axis_index(("x", "y_hi"))
    place = lax.axis_index(("z", "y_lo", "core"))
    base = (document * 32 + place) * SPANS
    maxsim, paired = scores(
        base.reshape(1), valid_len, keep, got, c_turned, growth, y_local, gate,
        norm_gain.reshape(1, INNER), w_head, q, pair_ids.reshape(1, QTOT),
    )
    everything = lax.all_to_all(paired, ("z", "y_lo", "core", "x", "y_hi"), 0, 0, tiled=True)
    return maxsim[None], jnp.sum(everything, axis=0)


def solution(mesh):
    cut = Mesh(mesh.devices.reshape(8, 2, 2, 4, 2), ("z", "y_lo", "core", "x", "y_hi"))
    seq, qry = ("z", "y_lo", "core"), ("x", "y_hi")
    return jax.shard_map(
        on_device,
        mesh=cut,
        in_specs=(
            P(qry, seq, None),
            P(qry, seq, None),
            P(qry, seq, None),
            P(qry, seq, None),
            P(qry, None, seq),
            P(),
            P(),
            P(),
            P(qry, None, None),
            P(qry, seq),
            P(),
        ),
        out_specs=(P(qry, seq, None), P()),
        check_vma=False,
    )
```

```python
import functools

import jax
import jax.numpy as jnp
from jax import lax
from jax.experimental import pallas as pl
from jax.experimental.pallas import tpu as pltpu
from jax.sharding import Mesh
from jax.sharding import PartitionSpec as P

HEADS = 32
HEAD_DIM = 64
STATE = 128
SPAN = 128
TOKENS = 1024
SPANS = TOKENS // SPAN
INNER = HEADS * HEAD_DIM
PAIRS = HEADS // 2
WIDE = 512
CHUNKS = INNER // WIDE
HALF = STATE // 2
ROWS = HALF + 16
QTOK = 32
QTOT = 128
EMB = 128
BLOCK = 256
TOGETHER = 2
F32 = jnp.float32
BF16 = jnp.bfloat16
NT = (((1,), (1,)), ((), ()))


def dot(a, b):
    return jnp.dot(a, b, preferred_element_type=F32)


def dot_nt(a, b):
    return lax.dot_general(a, b, NT, preferred_element_type=F32)


def iota(shape, dim):
    return lax.broadcasted_iota(jnp.int32, shape, dim)


def ones_where(cond):
    return jnp.where(cond, 1.0, 0.0).astype(BF16)


def split2(v):
    high = v.astype(BF16)
    return high, (v - high.astype(F32)).astype(BF16)


def split3(v):
    high = v.astype(BF16)
    rest = v - high.astype(F32)
    mid = rest.astype(BF16)
    return high, mid, (rest - mid.astype(F32)).astype(BF16)


def head_selector(rows, first_head, columns):
    head = iota((rows, columns), 0) & (HEADS - 1)
    return ones_where(head == first_head + (iota((rows, columns), 1) >> 6))


def states_kernel(
    core_ref, dec_any, b_any, x_any, keep_ref, send_ref, dec_ref, b_ref, x_ref, w_ref, bt_ref, sems
):
    get_dec = pltpu.make_async_copy(dec_any, dec_ref, sems.at[CHUNKS])
    get_b = pltpu.make_async_copy(b_any, b_ref, sems.at[CHUNKS + 1])
    get_x = [
        pltpu.make_async_copy(x_any.at[:, j * WIDE : (j + 1) * WIDE], x_ref.at[j], sems.at[j])
        for j in range(CHUNKS)
    ]
    for copy in (get_dec, get_b, *get_x):
        copy.start()
    row, col = iota((SPAN + 16, SPAN), 0), iota((SPAN + 16, SPAN), 1)
    after = ones_where((col > row) | (row >= SPAN))
    after = jnp.concatenate([after, after, after], axis=1)
    get_dec.wait()
    sums = [
        dot_nt(
            after,
            jnp.concatenate(
                split3(jnp.log2(dec_ref[:, c * SPAN : (c + 1) * SPAN])), axis=1
            ),
        )
        for c in range(SPANS)
    ]
    later = jnp.zeros((16, HEADS), F32)
    for c in reversed(range(SPANS)):
        high, low = split2(jnp.exp2(sums[c][:SPAN] + later[:1]))
        w_ref[c * SPAN : (c + 1) * SPAN, :] = jnp.concatenate([high, low], axis=1)
        later = later + sums[c][SPAN:]
    high, low = split2(jnp.exp2(later))
    place = iota((16, HEADS), 0)
    zero = jnp.zeros((16, HEADS), F32)
    decays = jnp.where(
        place == 0, high.astype(F32), jnp.where(place == 1, low.astype(F32), zero)
    ).astype(BF16)
    get_b.wait()
    for c in range(SPANS):
        rows = slice(c * SPAN, (c + 1) * SPAN)
        bt_ref[:, rows] = b_ref[rows, :].T
    lower = core_ref[0] == 0
    for j in range(CHUNKS):
        selector = head_selector(2 * HEADS, j * (WIDE // HEAD_DIM), WIDE)
        decay = dot(decays, selector[:HEADS]).astype(BF16)
        spread_out = dot(w_ref[...], selector)
        get_x[j].wait()
        weighted = (x_ref[j].astype(F32) * spread_out).astype(BF16)
        state = dot(bt_ref[...], weighted)
        mine = jnp.where(lower, state[:HALF], state[HALF:]).astype(BF16)
        other = jnp.where(lower, state[HALF:], state[:HALF]).astype(BF16)
        for k in range(WIDE // 128):
            lanes = slice(k * 128, (k + 1) * 128)
            pair = j * (WIDE // 128) + k
            keep_ref[pair, :HALF, :] = mine[:, lanes]
            keep_ref[pair, HALF:, :] = decay[:, lanes]
            send_ref[pair, :HALF, :] = other[:, lanes]
            send_ref[pair, HALF:, :] = decay[:, lanes]


def local_kernel(
    dec_ref, b_ref, c_ref, x_ref, skip_ref, y_ref, g_ref,
    carry_ref, e_ref, cum_ref, rows_ref, factor_ref
):
    step = pl.program_id(0)
    row, col = iota((SPAN, SPAN), 0), iota((SPAN, SPAN), 1)

    @pl.when(step == 0)
    def _():
        carry_ref[...] = jnp.zeros_like(carry_ref)
        e_ref[...] = head_selector(2 * HEADS, 0, INNER)
        until = ones_where(col <= row)
        after = ones_where(col > row)
        sums_of = jnp.concatenate([until, after, jnp.ones((16, SPAN), BF16)], axis=0)
        sums_of = jnp.concatenate([sums_of, sums_of, sums_of], axis=1)
        rows_until = ones_where(row <= col)
        rows_until = jnp.concatenate([rows_until, rows_until, rows_until], axis=0)
        prior = jnp.zeros((1, HEADS), F32)
        for c in range(SPANS):
            logs = jnp.log2(dec_ref[:, c * SPAN : (c + 1) * SPAN])
            logs = jnp.concatenate(split3(logs), axis=1)
            sums = dot_nt(sums_of, logs)
            cum_ref[c] = sums[:SPAN]
            rows_ref[c] = dot(logs, rows_until)
            high, low = split2(jnp.exp2(sums[:SPAN] + prior))
            g_ref[c * SPAN : (c + 1) * SPAN, :] = jnp.concatenate([high, low], axis=1)
            prior = prior + sums[2 * SPAN : 2 * SPAN + 1]
            factor_ref[c] = jnp.concatenate(split2(jnp.exp2(sums)), axis=1)

    left = col < HEAD_DIM
    for u in range(TOGETHER):
        span = step * TOGETHER + u
        here = slice(u * SPAN, (u + 1) * SPAN)
        cum, cum_rows, factors = cum_ref[span], rows_ref[span], factor_ref[span]
        c_span, b_span = c_ref[here, :], b_ref[here, :]
        b_turned = b_span.T
        cross = jnp.where(col <= row, dot_nt(c_span, b_span), 0.0)
        for j in range(CHUNKS):
            wide = slice(j * WIDE, (j + 1) * WIDE)
            spread_out = dot(factors, e_ref[:, wide])
            carry = carry_ref[:, wide]
            read = dot(c_span, carry.astype(BF16)) * spread_out[:SPAN]
            x_wide = x_ref[here, wide].astype(F32)
            parts = []
            for k in range(WIDE // 128):
                mixes = []
                for h in (j * 8 + 2 * k, j * 8 + 2 * k + 1):
                    spread = jnp.minimum(cum[:, h : h + 1] - cum_rows[h : h + 1, :], 0.0)
                    mixes.append((jnp.exp2(spread) * cross).astype(BF16))
                x_pair = x_ref[here, j * WIDE + k * 128 : j * WIDE + (k + 1) * 128]
                none = jnp.zeros_like(x_pair)
                x_both = jnp.concatenate(
                    [jnp.where(left, x_pair, none), jnp.where(left, none, x_pair)], axis=0
                )
                parts.append(dot(jnp.concatenate(mixes, axis=1), x_both))
            y = jnp.concatenate(parts, axis=1) + read + skip_ref[:, wide] * x_wide
            y_ref[here, wide] = y.astype(BF16)
            weighted = (x_wide * spread_out[SPAN : 2 * SPAN]).astype(BF16)
            carry_ref[:, wide] = spread_out[2 * SPAN : 2 * SPAN + 1] * carry + dot(b_turned, weighted)


def scan_kernel(in_ref, out_ref):
    carry = jnp.zeros((HALF, 128), F32)
    for k in range(PAIRS):
        out_ref[k] = carry.astype(BF16)
        decay = in_ref[k, HALF : HALF + 8, :].astype(F32)
        decay = decay[0:1] + decay[1:2]
        carry = decay * carry + in_ref[k, :HALF, :].astype(F32)


def score_kernel(
    base_ref, valid_ref, keep_ref, got_ref, c_ref, g_ref, y_any, z_any, gain_ref, head_ref,
    q0_ref, q1_ref, q2_ref, q3_ref, pair_ref, score_ref, paired_ref,
    e_ref, mean_ref, best_ref, enter_ref, q_ref, y_ref, z_ref, sems
):
    step = pl.program_id(0)

    def fetches(i):
        rows = pl.ds(i * BLOCK, BLOCK)
        return (
            pltpu.make_async_copy(y_any.at[rows, :], y_ref.at[i], sems.at[0, i]),
            pltpu.make_async_copy(z_any.at[rows, :], z_ref.at[i], sems.at[1, i]),
        )

    @pl.when(step == 0)
    def _():
        for i in range(TOKENS // BLOCK):
            for fetch in fetches(i):
                fetch.start()
        e_ref[...] = head_selector(2 * HEADS, 0, INNER)
        same = (iota((256, 256), 0) >> 6) == (iota((256, 256), 1) >> 6)
        mean_ref[...] = jnp.where(same, 1.0 / HEAD_DIM, 0.0).astype(BF16)
        for d in range(8):
            place = pl.multiple_of((base_ref[2] ^ d) * 16, 16)
            part = (q0_ref, q1_ref, q2_ref, q3_ref)[d // 2]
            for i in range(QTOK):
                q_ref[pl.ds(pl.multiple_of(i * QTOT + place, 16), 16), :] = part[d % 2, i]
        lower = base_ref[1] == 0
        for k in range(PAIRS):
            lanes = slice(k * 128, (k + 1) * 128)
            keep, got = keep_ref[k].astype(F32), got_ref[k].astype(F32)
            enter_ref[:HALF, lanes] = jnp.where(lower, keep, got).astype(BF16)
            enter_ref[HALF:, lanes] = jnp.where(lower, got, keep).astype(BF16)

    for fetch in fetches(step):
        fetch.wait()
    factors, c_part = g_ref[...], c_ref[...]
    embedded = jnp.zeros((BLOCK, EMB), F32)
    for j in range(2):
        wide = slice(j * INNER // 2, (j + 1) * INNER // 2)
        y = y_ref[step, :, wide].astype(F32) + dot(factors, e_ref[:, wide]) * dot(c_part, enter_ref[:, wide])
        z_half = 0.5 * z_ref[step, :, wide].astype(F32)
        gated = y * (z_half + z_half * jnp.tanh(z_half))
        squares = (gated * gated).astype(BF16)
        means = jnp.concatenate(
            [dot(squares[:, k : k + 256], mean_ref[...]) for k in range(0, INNER // 2, 256)], axis=1
        )
        normed = (gated * lax.rsqrt(means + 1e-05) * gain_ref[:, wide]).astype(BF16)
        embedded = embedded + dot(normed, head_ref[wide, :])
    embedded = embedded * lax.rsqrt(jnp.sum(embedded * embedded, axis=1, keepdims=True) + 1e-06)
    for p in range(BLOCK // SPAN):
        passage = step * (BLOCK // SPAN) + p
        vectors = embedded[p * SPAN : (p + 1) * SPAN]
        kept = iota((SPAN, EMB), 0) < valid_ref[0, passage]
        vectors = jnp.where(kept, vectors, vectors[:1]).astype(BF16)
        for j in range(QTOK * QTOT // 1024):
            lanes = slice(j * 1024, (j + 1) * 1024)
            sims = dot_nt(vectors, q_ref[lanes, :])
            best_ref[pl.ds(passage, 1), lanes] = jnp.max(sims, axis=0, keepdims=True)

    @pl.when(step == TOKENS // BLOCK - 1)
    def _():
        total = best_ref[:, :QTOT]
        for i in range(1, QTOK):
            total = total + best_ref[:, i * QTOT : (i + 1) * QTOT]
        score_ref[...] = total
        matched = pair_ref[...] == base_ref[0] + iota((SPANS, QTOT), 0)
        paired = jnp.sum(jnp.where(matched, total, 0.0), axis=0, keepdims=True)
        paired_ref[...] = jnp.broadcast_to(paired, paired_ref.shape)


def whole(shape, space=None):
    kind = {} if space is None else {"memory_space": space}
    return pl.BlockSpec(shape, lambda i: (0,) * len(shape), **kind)


def params(mib):
    return pltpu.CompilerParams(
        dimension_semantics=("arbitrary",), vmem_limit_bytes=mib * 1024 * 1024
    )


def cost(flops, bytes_accessed, transcendentals=0):
    return pl.CostEstimate(
        flops=flops, bytes_accessed=bytes_accessed, transcendentals=transcendentals
    )


def device_states(core, decays, b, x):
    packed = jax.ShapeDtypeStruct((PAIRS, ROWS, 128), BF16)
    far = pl.BlockSpec(memory_space=pltpu.HBM)
    near = pl.BlockSpec(memory_space=pltpu.VMEM)
    return pl.pallas_call(
        states_kernel,
        in_specs=[pl.BlockSpec(memory_space=pltpu.SMEM), far, far, far],
        out_specs=[near, near],
        out_shape=[packed, packed],
        scratch_shapes=[
            pltpu.VMEM((HEADS, TOKENS), F32),
            pltpu.VMEM((TOKENS, STATE), BF16),
            pltpu.VMEM((CHUNKS, TOKENS, WIDE), BF16),
            pltpu.VMEM((TOKENS, 2 * HEADS), BF16),
            pltpu.VMEM((STATE, TOKENS), BF16),
            pltpu.SemaphoreType.DMA((CHUNKS + 2,)),
        ],
        compiler_params=pltpu.CompilerParams(vmem_limit_bytes=60 * 1024 * 1024),
        cost_estimate=cost(10**9, 5 * 10**6),
        name="device_states",
    )(core, decays, b, x)


def local_part(decays, b, c, x, skip):
    def tokens(columns):
        return pl.BlockSpec((TOGETHER * SPAN, columns), lambda i: (i, 0))

    return pl.pallas_call(
        local_kernel,
        grid=(SPANS // TOGETHER,),
        in_specs=[
            whole((HEADS, TOKENS)),
            tokens(STATE),
            tokens(STATE),
            tokens(INNER),
            whole((1, INNER)),
        ],
        out_specs=[tokens(INNER), whole((TOKENS, 2 * HEADS))],
        out_shape=[
            jax.ShapeDtypeStruct((TOKENS, INNER), BF16),
            jax.ShapeDtypeStruct((TOKENS, 2 * HEADS), BF16),
        ],
        scratch_shapes=[
            pltpu.VMEM((STATE, INNER), F32),
            pltpu.VMEM((2 * HEADS, INNER), BF16),
            pltpu.VMEM((SPANS, SPAN, HEADS), F32),
            pltpu.VMEM((SPANS, HEADS, SPAN), F32),
            pltpu.VMEM((SPANS, 2 * SPAN + 16, 2 * HEADS), BF16),
        ],
        compiler_params=params(60),
        cost_estimate=cost(8 * 10**9, 9 * 10**6, 4 * 10**6),
        name="local_part",
    )(decays, b, c, x, skip)


def scan_chips(states):
    return pl.pallas_call(
        scan_kernel,
        out_shape=jax.ShapeDtypeStruct((PAIRS, HALF, 128), BF16),
        compiler_params=pltpu.CompilerParams(vmem_limit_bytes=4 * 1024 * 1024),
        cost_estimate=cost(10**6, 600_000),
        name="scan_chips",
    )(states)


def scores(base, valid_len, keep, got, c, growth, y, z, gain, w_head, q, pair_ids):
    def tokens(width):
        return pl.BlockSpec((BLOCK, width), lambda i: (i, 0))

    smem = pl.BlockSpec(memory_space=pltpu.SMEM)
    far = pl.BlockSpec(memory_space=pltpu.HBM)
    half = whole((PAIRS, HALF, 128))
    everyone = 256
    return pl.pallas_call(
        score_kernel,
        grid=(TOKENS // BLOCK,),
        in_specs=[
            smem,
            smem,
            half,
            half,
            tokens(STATE),
            tokens(2 * HEADS),
            far,
            far,
            whole((1, INNER)),
            whole((INNER, EMB)),
            *[whole((2, QTOK, QTOT // 8, EMB))] * 4,
            whole((1, QTOT)),
        ],
        out_specs=[whole((SPANS, QTOT)), whole((everyone, QTOT))],
        out_shape=[
            jax.ShapeDtypeStruct((SPANS, QTOT), F32),
            jax.ShapeDtypeStruct((everyone, QTOT), F32),
        ],
        scratch_shapes=[
            pltpu.VMEM((2 * HEADS, INNER), BF16),
            pltpu.VMEM((256, 256), BF16),
            pltpu.VMEM((SPANS, QTOK * QTOT), F32),
            pltpu.VMEM((STATE, INNER), BF16),
            pltpu.VMEM((QTOK * QTOT, EMB), BF16),
            pltpu.VMEM((TOKENS // BLOCK, BLOCK, INNER), BF16),
            pltpu.VMEM((TOKENS // BLOCK, BLOCK, INNER), BF16),
            pltpu.SemaphoreType.DMA((2, TOKENS // BLOCK)),
        ],
        compiler_params=params(60),
        cost_estimate=cost(6 * 10**9, 11 * 10**6, 2 * 10**6),
        name="scores",
    )(base, valid_len, keep, got, c, growth, y, z, gain, w_head, *q, pair_ids)


def swap_cores(v):
    return lax.ppermute(v, "core", [(0, 1), (1, 0)])


def decay_of(packed):
    return packed[:, HALF : HALF + 1].astype(F32) + packed[:, HALF + 1 : HALF + 2].astype(F32)


def on_device(
    x_inner, z_gate, b_proj, c_proj, decays, d_skip, norm_gain, w_head, queries, valid_len, pair_ids
):
    core = lax.axis_index("core")
    x, z, b, c, decay = x_inner[0], z_gate[0], b_proj[0], c_proj[0], decays[0]

    own, send = device_states(core.reshape(1), decay, b, x)
    got = swap_cores(send)
    lower = core == 0
    first = jnp.where(lower, own, got)
    second = jnp.where(lower, got, own)
    d_first, d_second = decay_of(first), decay_of(second)
    chip = d_second * first[:, :HALF].astype(F32) + second[:, :HALF].astype(F32)
    high, low = split2(d_first * d_second)
    fill = jnp.zeros((PAIRS, 14, 128), BF16)
    packed = jnp.concatenate([chip.astype(BF16), high, low, fill], axis=1)
    packed, decay, queries = lax.optimization_barrier((packed, decay, queries))
    by_pair = lax.all_to_all(packed, ("z", "y_lo"), 0, 0, tiled=True)

    wide = queries.astype(F32)
    q = (wide * lax.rsqrt(jnp.sum(wide * wide, axis=-1, keepdims=True) + 1e-06)).astype(BF16)
    q = lax.optimization_barrier(q.transpose(1, 0, 2))
    q_pair = jnp.stack([q, lax.ppermute(q, "y_hi", [(0, 1), (1, 0)])])
    document = lax.axis_index(("x", "y_hi"))
    place = lax.axis_index(("z", "y_lo", "core"))
    base = jnp.stack([(document * 32 + place) * SPANS, core, document])
    skip = jnp.repeat(d_skip, HEAD_DIM).reshape(1, INNER)
    y, growth = local_part(decay, b, c, x, skip)
    by_pair, y, growth, q_pair, base = lax.optimization_barrier(
        (by_pair, y, growth, q_pair, base)
    )
    prefix, q_pair = lax.optimization_barrier((scan_chips(by_pair), q_pair))
    entering = lax.all_to_all(prefix, ("z", "y_lo"), 0, 0, tiled=True)
    q_parts = [q_pair] + [
        lax.ppermute(q_pair, "x", [(i, i ^ d) for i in range(4)]) for d in range(1, 4)
    ]
    after = (
        d_first * entering.astype(F32) + first[:, :HALF].astype(F32)
    ).astype(BF16)
    keep = jnp.where(lower, entering, after)
    got = swap_cores(jnp.where(lower, after, entering))

    maxsim, paired = scores(
        base, valid_len, keep, got, c, growth, y, z, norm_gain.reshape(1, INNER), w_head, q_parts,
        pair_ids.reshape(1, QTOT),
    )
    everything = lax.all_to_all(paired, ("z", "y_lo", "core", "x", "y_hi"), 0, 0, tiled=True)
    return maxsim[None], jnp.sum(everything, axis=0)


def solution(mesh):
    cut = Mesh(mesh.devices.reshape(8, 2, 2, 4, 2), ("z", "y_lo", "core", "x", "y_hi"))
    seq, qry = ("z", "y_lo", "core"), ("x", "y_hi")
    return jax.shard_map(
        on_device,
        mesh=cut,
        in_specs=(
            P(qry, seq, None),
            P(qry, seq, None),
            P(qry, seq, None),
            P(qry, seq, None),
            P(qry, None, seq),
            P(),
            P(),
            P(),
            P(qry, None, None),
            P(qry, seq),
            P(),
        ),
        out_specs=(P(qry, seq, None), P()),
        check_vma=False,
    )
```

```python
import functools

import jax
import jax.numpy as jnp
from jax import lax
from jax.experimental import pallas as pl
from jax.experimental.pallas import tpu as pltpu
from jax.sharding import Mesh
from jax.sharding import PartitionSpec as P

HEADS = 32
HEAD_DIM = 64
STATE = 128
SPAN = 128
TOKENS = 1024
SPANS = TOKENS // SPAN
INNER = HEADS * HEAD_DIM
PAIRS = HEADS // 2
WIDE = 512
CHUNKS = INNER // WIDE
HALF = STATE // 2
ROWS = HALF + 16
QTOK = 32
QTOT = 128
EMB = 128
BLOCK = 256
TOGETHER = 2
F32 = jnp.float32
BF16 = jnp.bfloat16
NT = (((1,), (1,)), ((), ()))


def dot(a, b):
    return jnp.dot(a, b, preferred_element_type=F32)


def dot_nt(a, b):
    return lax.dot_general(a, b, NT, preferred_element_type=F32)


def iota(shape, dim):
    return lax.broadcasted_iota(jnp.int32, shape, dim)


def ones_where(cond):
    return jnp.where(cond, 1.0, 0.0).astype(BF16)


def split2(v):
    high = v.astype(BF16)
    return high, (v - high.astype(F32)).astype(BF16)


def split3(v):
    high = v.astype(BF16)
    rest = v - high.astype(F32)
    mid = rest.astype(BF16)
    return high, mid, (rest - mid.astype(F32)).astype(BF16)


def head_selector(rows, first_head, columns):
    head = iota((rows, columns), 0) & (HEADS - 1)
    return ones_where(head == first_head + (iota((rows, columns), 1) >> 6))


def states_kernel(
    core_ref, dec_any, b_any, x_any, keep_ref, send_ref, dec_ref, b_ref, x_ref, w_ref, bt_ref, sems
):
    get_dec = pltpu.make_async_copy(dec_any, dec_ref, sems.at[CHUNKS])
    get_b = pltpu.make_async_copy(b_any, b_ref, sems.at[CHUNKS + 1])
    get_x = [
        pltpu.make_async_copy(x_any.at[:, j * WIDE : (j + 1) * WIDE], x_ref.at[j], sems.at[j])
        for j in range(CHUNKS)
    ]
    for copy in (get_dec, get_b, *get_x):
        copy.start()
    row, col = iota((SPAN + 16, SPAN), 0), iota((SPAN + 16, SPAN), 1)
    after = ones_where((col > row) | (row >= SPAN))
    after = jnp.concatenate([after, after, after], axis=1)
    get_dec.wait()
    sums = [
        dot_nt(
            after,
            jnp.concatenate(
                split3(jnp.log2(dec_ref[:, c * SPAN : (c + 1) * SPAN])), axis=1
            ),
        )
        for c in range(SPANS)
    ]
    later = jnp.zeros((16, HEADS), F32)
    for c in reversed(range(SPANS)):
        high, low = split2(jnp.exp2(sums[c][:SPAN] + later[:1]))
        w_ref[c * SPAN : (c + 1) * SPAN, :] = jnp.concatenate([high, low], axis=1)
        later = later + sums[c][SPAN:]
    high, low = split2(jnp.exp2(later))
    place = iota((16, HEADS), 0)
    zero = jnp.zeros((16, HEADS), F32)
    decays = jnp.where(
        place == 0, high.astype(F32), jnp.where(place == 1, low.astype(F32), zero)
    ).astype(BF16)
    get_b.wait()
    for c in range(SPANS):
        rows = slice(c * SPAN, (c + 1) * SPAN)
        bt_ref[:, rows] = b_ref[rows, :].T
    lower = core_ref[0] == 0
    for j in range(CHUNKS):
        selector = head_selector(2 * HEADS, j * (WIDE // HEAD_DIM), WIDE)
        decay = dot(decays, selector[:HEADS]).astype(BF16)
        spread_out = dot(w_ref[...], selector)
        get_x[j].wait()
        weighted = (x_ref[j].astype(F32) * spread_out).astype(BF16)
        state = dot(bt_ref[...], weighted)
        mine = jnp.where(lower, state[:HALF], state[HALF:]).astype(BF16)
        other = jnp.where(lower, state[HALF:], state[:HALF]).astype(BF16)
        for k in range(WIDE // 128):
            lanes = slice(k * 128, (k + 1) * 128)
            pair = j * (WIDE // 128) + k
            keep_ref[pair, :HALF, :] = mine[:, lanes]
            keep_ref[pair, HALF:, :] = decay[:, lanes]
            send_ref[pair, :HALF, :] = other[:, lanes]
            send_ref[pair, HALF:, :] = decay[:, lanes]


def local_kernel(
    dec_ref, b_ref, c_ref, x_ref, skip_ref, y_ref, g_ref,
    carry_ref, e_ref, cum_ref, rows_ref, factor_ref
):
    step = pl.program_id(0)
    row, col = iota((SPAN, SPAN), 0), iota((SPAN, SPAN), 1)

    @pl.when(step == 0)
    def _():
        carry_ref[...] = jnp.zeros_like(carry_ref)
        e_ref[...] = head_selector(2 * HEADS, 0, INNER)
        until = ones_where(col <= row)
        after = ones_where(col > row)
        sums_of = jnp.concatenate([until, after, jnp.ones((16, SPAN), BF16)], axis=0)
        sums_of = jnp.concatenate([sums_of, sums_of, sums_of], axis=1)
        rows_until = ones_where(row <= col)
        rows_until = jnp.concatenate([rows_until, rows_until, rows_until], axis=0)
        prior = jnp.zeros((1, HEADS), F32)
        for c in range(SPANS):
            logs = jnp.log2(dec_ref[:, c * SPAN : (c + 1) * SPAN])
            logs = jnp.concatenate(split3(logs), axis=1)
            sums = dot_nt(sums_of, logs)
            cum_ref[c] = sums[:SPAN]
            rows_ref[c] = dot(logs, rows_until)
            high, low = split2(jnp.exp2(sums[:SPAN] + prior))
            g_ref[c * SPAN : (c + 1) * SPAN, :] = jnp.concatenate([high, low], axis=1)
            prior = prior + sums[2 * SPAN : 2 * SPAN + 1]
            factor_ref[c] = jnp.concatenate(split2(jnp.exp2(sums)), axis=1)

    left = col < HEAD_DIM
    for u in range(TOGETHER):
        span = step * TOGETHER + u
        here = slice(u * SPAN, (u + 1) * SPAN)
        cum, cum_rows, factors = cum_ref[span], rows_ref[span], factor_ref[span]
        c_span, b_span = c_ref[here, :], b_ref[here, :]
        b_turned = b_span.T
        cross = jnp.where(col <= row, dot_nt(c_span, b_span), 0.0)
        for j in range(CHUNKS):
            wide = slice(j * WIDE, (j + 1) * WIDE)
            spread_out = dot(factors, e_ref[:, wide])
            carry = carry_ref[:, wide]
            read = dot(c_span, carry.astype(BF16)) * spread_out[:SPAN]
            x_wide = x_ref[here, wide].astype(F32)
            parts = []
            for k in range(WIDE // 128):
                mixes = []
                for h in (j * 8 + 2 * k, j * 8 + 2 * k + 1):
                    spread = jnp.minimum(cum[:, h : h + 1] - cum_rows[h : h + 1, :], 0.0)
                    mixes.append((jnp.exp2(spread) * cross).astype(BF16))
                x_pair = x_ref[here, j * WIDE + k * 128 : j * WIDE + (k + 1) * 128]
                none = jnp.zeros_like(x_pair)
                x_both = jnp.concatenate(
                    [jnp.where(left, x_pair, none), jnp.where(left, none, x_pair)], axis=0
                )
                parts.append(dot(jnp.concatenate(mixes, axis=1), x_both))
            y = jnp.concatenate(parts, axis=1) + read + skip_ref[:, wide] * x_wide
            y_ref[here, wide] = y.astype(BF16)
            weighted = (x_wide * spread_out[SPAN : 2 * SPAN]).astype(BF16)
            carry_ref[:, wide] = spread_out[2 * SPAN : 2 * SPAN + 1] * carry + dot(b_turned, weighted)


def scan_kernel(in_ref, out_ref):
    carry = jnp.zeros((HALF, 128), F32)
    for k in range(PAIRS):
        out_ref[k] = carry.astype(BF16)
        decay = in_ref[k, HALF : HALF + 8, :].astype(F32)
        decay = decay[0:1] + decay[1:2]
        carry = decay * carry + in_ref[k, :HALF, :].astype(F32)


def score_kernel(
    base_ref, valid_ref, keep_ref, got_ref, c_ref, g_ref, y_any, z_any, gain_ref, head_ref,
    q0_ref, q1_ref, q2_ref, q3_ref, pair_ref, score_ref, paired_ref,
    e_ref, mean_ref, best_ref, enter_ref, q_ref, y_ref, z_ref, sems
):
    step = pl.program_id(0)

    def fetches(i):
        rows = pl.ds(i * BLOCK, BLOCK)
        return (
            pltpu.make_async_copy(y_any.at[rows, :], y_ref.at[i], sems.at[0, i]),
            pltpu.make_async_copy(z_any.at[rows, :], z_ref.at[i], sems.at[1, i]),
        )

    @pl.when(step == 0)
    def _():
        for i in range(TOKENS // BLOCK):
            for fetch in fetches(i):
                fetch.start()
        e_ref[...] = head_selector(2 * HEADS, 0, INNER)
        same = (iota((256, 256), 0) >> 6) == (iota((256, 256), 1) >> 6)
        mean_ref[...] = jnp.where(same, 1.0 / HEAD_DIM, 0.0).astype(BF16)
        for d in range(8):
            place = pl.multiple_of((base_ref[2] ^ d) * 16, 16)
            part = (q0_ref, q1_ref, q2_ref, q3_ref)[d // 2]
            for i in range(QTOK):
                q_ref[pl.ds(pl.multiple_of(i * QTOT + place, 16), 16), :] = part[d % 2, i]
        lower = base_ref[1] == 0
        for k in range(PAIRS):
            lanes = slice(k * 128, (k + 1) * 128)
            keep, got = keep_ref[k].astype(F32), got_ref[k].astype(F32)
            enter_ref[:HALF, lanes] = jnp.where(lower, keep, got).astype(BF16)
            enter_ref[HALF:, lanes] = jnp.where(lower, got, keep).astype(BF16)

    for fetch in fetches(step):
        fetch.wait()
    factors, c_part = g_ref[...], c_ref[...]
    embedded = jnp.zeros((BLOCK, EMB), F32)
    for j in range(2):
        wide = slice(j * INNER // 2, (j + 1) * INNER // 2)
        y = y_ref[step, :, wide].astype(F32) + dot(factors, e_ref[:, wide]) * dot(c_part, enter_ref[:, wide])
        z_half = 0.5 * z_ref[step, :, wide].astype(F32)
        gated = y * (z_half + z_half * jnp.tanh(z_half))
        squares = (gated * gated).astype(BF16)
        means = jnp.concatenate(
            [dot(squares[:, k : k + 256], mean_ref[...]) for k in range(0, INNER // 2, 256)], axis=1
        )
        normed = (gated * lax.rsqrt(means + 1e-05) * gain_ref[:, wide]).astype(BF16)
        embedded = embedded + dot(normed, head_ref[wide, :])
    embedded = embedded * lax.rsqrt(jnp.sum(embedded * embedded, axis=1, keepdims=True) + 1e-06)
    for p in range(BLOCK // SPAN):
        passage = step * (BLOCK // SPAN) + p
        vectors = embedded[p * SPAN : (p + 1) * SPAN]
        kept = iota((SPAN, EMB), 0) < valid_ref[0, passage]
        vectors = jnp.where(kept, vectors, vectors[:1]).astype(BF16)
        for j in range(QTOK * QTOT // 1024):
            lanes = slice(j * 1024, (j + 1) * 1024)
            sims = dot_nt(vectors, q_ref[lanes, :])
            best_ref[pl.ds(passage, 1), lanes] = jnp.max(sims, axis=0, keepdims=True)

    @pl.when(step == TOKENS // BLOCK - 1)
    def _():
        total = best_ref[:, :QTOT]
        for i in range(1, QTOK):
            total = total + best_ref[:, i * QTOT : (i + 1) * QTOT]
        score_ref[...] = total
        matched = pair_ref[...] == base_ref[0] + iota((SPANS, QTOT), 0)
        paired = jnp.sum(jnp.where(matched, total, 0.0), axis=0, keepdims=True)
        paired_ref[...] = jnp.broadcast_to(paired, paired_ref.shape)


def whole(shape, space=None):
    kind = {} if space is None else {"memory_space": space}
    return pl.BlockSpec(shape, lambda i: (0,) * len(shape), **kind)


def params(mib):
    return pltpu.CompilerParams(
        dimension_semantics=("arbitrary",), vmem_limit_bytes=mib * 1024 * 1024
    )


def cost(flops, bytes_accessed, transcendentals=0):
    return pl.CostEstimate(
        flops=flops, bytes_accessed=bytes_accessed, transcendentals=transcendentals
    )


def device_states(core, decays, b, x):
    packed = jax.ShapeDtypeStruct((PAIRS, ROWS, 128), BF16)
    far = pl.BlockSpec(memory_space=pltpu.HBM)
    near = pl.BlockSpec(memory_space=pltpu.VMEM)
    return pl.pallas_call(
        states_kernel,
        in_specs=[pl.BlockSpec(memory_space=pltpu.SMEM), far, far, far],
        out_specs=[near, near],
        out_shape=[packed, packed],
        scratch_shapes=[
            pltpu.VMEM((HEADS, TOKENS), F32),
            pltpu.VMEM((TOKENS, STATE), BF16),
            pltpu.VMEM((CHUNKS, TOKENS, WIDE), BF16),
            pltpu.VMEM((TOKENS, 2 * HEADS), BF16),
            pltpu.VMEM((STATE, TOKENS), BF16),
            pltpu.SemaphoreType.DMA((CHUNKS + 2,)),
        ],
        compiler_params=pltpu.CompilerParams(vmem_limit_bytes=60 * 1024 * 1024),
        cost_estimate=cost(10**9, 5 * 10**6),
        name="device_states",
    )(core, decays, b, x)


def local_part(decays, b, c, x, skip):
    def tokens(columns):
        return pl.BlockSpec((TOGETHER * SPAN, columns), lambda i: (i, 0))

    return pl.pallas_call(
        local_kernel,
        grid=(SPANS // TOGETHER,),
        in_specs=[
            whole((HEADS, TOKENS)),
            tokens(STATE),
            tokens(STATE),
            tokens(INNER),
            whole((1, INNER)),
        ],
        out_specs=[tokens(INNER), whole((TOKENS, 2 * HEADS))],
        out_shape=[
            jax.ShapeDtypeStruct((TOKENS, INNER), BF16),
            jax.ShapeDtypeStruct((TOKENS, 2 * HEADS), BF16),
        ],
        scratch_shapes=[
            pltpu.VMEM((STATE, INNER), F32),
            pltpu.VMEM((2 * HEADS, INNER), BF16),
            pltpu.VMEM((SPANS, SPAN, HEADS), F32),
            pltpu.VMEM((SPANS, HEADS, SPAN), F32),
            pltpu.VMEM((SPANS, 2 * SPAN + 16, 2 * HEADS), BF16),
        ],
        compiler_params=params(60),
        cost_estimate=cost(8 * 10**9, 9 * 10**6, 4 * 10**6),
        name="local_part",
    )(decays, b, c, x, skip)


def scan_chips(states):
    return pl.pallas_call(
        scan_kernel,
        out_shape=jax.ShapeDtypeStruct((PAIRS, HALF, 128), BF16),
        compiler_params=pltpu.CompilerParams(vmem_limit_bytes=4 * 1024 * 1024),
        cost_estimate=cost(10**6, 600_000),
        name="scan_chips",
    )(states)


def scores(base, valid_len, keep, got, c, growth, y, z, gain, w_head, q, pair_ids):
    def tokens(width):
        return pl.BlockSpec((BLOCK, width), lambda i: (i, 0))

    smem = pl.BlockSpec(memory_space=pltpu.SMEM)
    far = pl.BlockSpec(memory_space=pltpu.HBM)
    half = whole((PAIRS, HALF, 128))
    everyone = 256
    return pl.pallas_call(
        score_kernel,
        grid=(TOKENS // BLOCK,),
        in_specs=[
            smem,
            smem,
            half,
            half,
            tokens(STATE),
            tokens(2 * HEADS),
            far,
            far,
            whole((1, INNER)),
            whole((INNER, EMB)),
            *[whole((2, QTOK, QTOT // 8, EMB))] * 4,
            whole((1, QTOT)),
        ],
        out_specs=[whole((SPANS, QTOT)), whole((everyone, QTOT))],
        out_shape=[
            jax.ShapeDtypeStruct((SPANS, QTOT), F32),
            jax.ShapeDtypeStruct((everyone, QTOT), F32),
        ],
        scratch_shapes=[
            pltpu.VMEM((2 * HEADS, INNER), BF16),
            pltpu.VMEM((256, 256), BF16),
            pltpu.VMEM((SPANS, QTOK * QTOT), F32),
            pltpu.VMEM((STATE, INNER), BF16),
            pltpu.VMEM((QTOK * QTOT, EMB), BF16),
            pltpu.VMEM((TOKENS // BLOCK, BLOCK, INNER), BF16),
            pltpu.VMEM((TOKENS // BLOCK, BLOCK, INNER), BF16),
            pltpu.SemaphoreType.DMA((2, TOKENS // BLOCK)),
        ],
        compiler_params=params(50),
        cost_estimate=cost(6 * 10**9, 11 * 10**6, 2 * 10**6),
        name="scores",
    )(base, valid_len, keep, got, c, growth, y, z, gain, w_head, *q, pair_ids)


def swap_cores(v):
    return lax.ppermute(v, "core", [(0, 1), (1, 0)])


def decay_of(packed):
    return packed[:, HALF : HALF + 1].astype(F32) + packed[:, HALF + 1 : HALF + 2].astype(F32)


def on_device(
    x_inner, z_gate, b_proj, c_proj, decays, d_skip, norm_gain, w_head, queries, valid_len, pair_ids
):
    core = lax.axis_index("core")
    x, z, b, c, decay = x_inner[0], z_gate[0], b_proj[0], c_proj[0], decays[0]

    own, send = device_states(core.reshape(1), decay, b, x)
    got = swap_cores(send)
    lower = core == 0
    first = jnp.where(lower, own, got)
    second = jnp.where(lower, got, own)
    d_first, d_second = decay_of(first), decay_of(second)
    chip = d_second * first[:, :HALF].astype(F32) + second[:, :HALF].astype(F32)
    high, low = split2(d_first * d_second)
    fill = jnp.zeros((PAIRS, 14, 128), BF16)
    packed = jnp.concatenate([chip.astype(BF16), high, low, fill], axis=1)
    packed, decay, queries, d_skip, own_core = lax.optimization_barrier(
        (packed, decay, queries, d_skip, core)
    )
    by_pair = lax.all_to_all(packed, ("z", "y_lo"), 0, 0, tiled=True)

    wide = queries.astype(F32)
    q = (wide * lax.rsqrt(jnp.sum(wide * wide, axis=-1, keepdims=True) + 1e-06)).astype(BF16)
    q = lax.optimization_barrier(q.transpose(1, 0, 2))
    q_pair = jnp.stack([q, lax.ppermute(q, "y_hi", [(0, 1), (1, 0)])])
    document = lax.axis_index(("x", "y_hi"))
    place = lax.axis_index(("z", "y_lo", "core"))
    base = jnp.stack([(document * 32 + place) * SPANS, own_core, document])
    skip = jnp.repeat(d_skip, HEAD_DIM).reshape(1, INNER)
    y, growth = local_part(decay, b, c, x, skip)
    by_pair, y, growth, q_pair, base = lax.optimization_barrier(
        (by_pair, y, growth, q_pair, base)
    )
    prefix, q_pair = lax.optimization_barrier((scan_chips(by_pair), q_pair))
    entering = lax.all_to_all(prefix, ("z", "y_lo"), 0, 0, tiled=True)
    q_parts = [q_pair] + [
        lax.ppermute(q_pair, "x", [(i, i ^ d) for i in range(4)]) for d in range(1, 4)
    ]
    after = (
        d_first * entering.astype(F32) + first[:, :HALF].astype(F32)
    ).astype(BF16)
    keep = jnp.where(lower, entering, after)
    got = swap_cores(jnp.where(lower, after, entering))

    maxsim, paired = scores(
        base, valid_len, keep, got, c, growth, y, z, norm_gain.reshape(1, INNER), w_head, q_parts,
        pair_ids.reshape(1, QTOT),
    )
    everything = lax.all_to_all(paired, ("z", "y_lo", "core", "x", "y_hi"), 0, 0, tiled=True)
    return maxsim[None], jnp.sum(everything, axis=0)


def solution(mesh):
    cut = Mesh(mesh.devices.reshape(8, 2, 2, 4, 2), ("z", "y_lo", "core", "x", "y_hi"))
    seq, qry = ("z", "y_lo", "core"), ("x", "y_hi")
    return jax.shard_map(
        on_device,
        mesh=cut,
        in_specs=(
            P(qry, seq, None),
            P(qry, seq, None),
            P(qry, seq, None),
            P(qry, seq, None),
            P(qry, None, seq),
            P(),
            P(),
            P(),
            P(qry, None, None),
            P(qry, seq),
            P(),
        ),
        out_specs=(P(qry, seq, None), P()),
        check_vma=False,
    )
```

```python
import functools

import jax
import jax.numpy as jnp
from jax import lax
from jax.experimental import pallas as pl
from jax.experimental.pallas import tpu as pltpu
from jax.sharding import Mesh
from jax.sharding import PartitionSpec as P

HEADS = 32
HEAD_DIM = 64
STATE = 128
SPAN = 128
TOKENS = 1024
SPANS = TOKENS // SPAN
INNER = HEADS * HEAD_DIM
PAIRS = HEADS // 2
WIDE = 512
CHUNKS = INNER // WIDE
HALF = STATE // 2
ROWS = HALF + 16
QTOK = 32
QTOT = 128
EMB = 128
BLOCK = 256
TOGETHER = 2
F32 = jnp.float32
BF16 = jnp.bfloat16
NT = (((1,), (1,)), ((), ()))


def dot(a, b):
    return jnp.dot(a, b, preferred_element_type=F32)


def dot_nt(a, b):
    return lax.dot_general(a, b, NT, preferred_element_type=F32)


def iota(shape, dim):
    return lax.broadcasted_iota(jnp.int32, shape, dim)


def ones_where(cond):
    return jnp.where(cond, 1.0, 0.0).astype(BF16)


def split2(v):
    high = v.astype(BF16)
    return high, (v - high.astype(F32)).astype(BF16)


def split3(v):
    high = v.astype(BF16)
    rest = v - high.astype(F32)
    mid = rest.astype(BF16)
    return high, mid, (rest - mid.astype(F32)).astype(BF16)


def head_selector(rows, first_head, columns):
    head = iota((rows, columns), 0) & (HEADS - 1)
    return ones_where(head == first_head + (iota((rows, columns), 1) >> 6))


def states_kernel(
    core_ref, dec_any, b_any, x_any, keep_ref, send_ref, dec_ref, b_ref, x_ref, w_ref, bt_ref, sems
):
    get_dec = pltpu.make_async_copy(dec_any, dec_ref, sems.at[CHUNKS])
    get_b = pltpu.make_async_copy(b_any, b_ref, sems.at[CHUNKS + 1])
    get_x = [
        pltpu.make_async_copy(x_any.at[:, j * WIDE : (j + 1) * WIDE], x_ref.at[j], sems.at[j])
        for j in range(CHUNKS)
    ]
    for copy in (get_dec, get_b, *get_x):
        copy.start()
    row, col = iota((SPAN + 16, SPAN), 0), iota((SPAN + 16, SPAN), 1)
    after = ones_where((col > row) | (row >= SPAN))
    after = jnp.concatenate([after, after, after], axis=1)
    get_dec.wait()
    sums = [
        dot_nt(
            after,
            jnp.concatenate(
                split3(jnp.log2(dec_ref[:, c * SPAN : (c + 1) * SPAN])), axis=1
            ),
        )
        for c in range(SPANS)
    ]
    later = jnp.zeros((16, HEADS), F32)
    for c in reversed(range(SPANS)):
        high, low = split2(jnp.exp2(sums[c][:SPAN] + later[:1]))
        w_ref[c * SPAN : (c + 1) * SPAN, :] = jnp.concatenate([high, low], axis=1)
        later = later + sums[c][SPAN:]
    high, low = split2(jnp.exp2(later))
    place = iota((16, HEADS), 0)
    zero = jnp.zeros((16, HEADS), F32)
    decays = jnp.where(
        place == 0, high.astype(F32), jnp.where(place == 1, low.astype(F32), zero)
    ).astype(BF16)
    get_b.wait()
    for c in range(SPANS):
        rows = slice(c * SPAN, (c + 1) * SPAN)
        bt_ref[:, rows] = b_ref[rows, :].T
    lower = core_ref[0] == 0
    for j in range(CHUNKS):
        selector = head_selector(2 * HEADS, j * (WIDE // HEAD_DIM), WIDE)
        decay = dot(decays, selector[:HEADS]).astype(BF16)
        spread_out = dot(w_ref[...], selector)
        get_x[j].wait()
        weighted = (x_ref[j].astype(F32) * spread_out).astype(BF16)
        state = dot(bt_ref[...], weighted)
        mine = jnp.where(lower, state[:HALF], state[HALF:]).astype(BF16)
        other = jnp.where(lower, state[HALF:], state[:HALF]).astype(BF16)
        for k in range(WIDE // 128):
            lanes = slice(k * 128, (k + 1) * 128)
            pair = j * (WIDE // 128) + k
            keep_ref[pair, :HALF, :] = mine[:, lanes]
            keep_ref[pair, HALF:, :] = decay[:, lanes]
            send_ref[pair, :HALF, :] = other[:, lanes]
            send_ref[pair, HALF:, :] = decay[:, lanes]


def local_kernel(
    first_head, dec_ref, b_ref, c_ref, x_ref, skip_ref, y_ref, g_ref,
    carry_ref, e_ref, cum_ref, rows_ref, factor_ref
):
    step = pl.program_id(0)
    row, col = iota((SPAN, SPAN), 0), iota((SPAN, SPAN), 1)

    @pl.when(step == 0)
    def _():
        carry_ref[...] = jnp.zeros_like(carry_ref)
        e_ref[...] = head_selector(2 * HEADS, first_head, INNER // 2)
        until = ones_where(col <= row)
        after = ones_where(col > row)
        sums_of = jnp.concatenate([until, after, jnp.ones((16, SPAN), BF16)], axis=0)
        sums_of = jnp.concatenate([sums_of, sums_of, sums_of], axis=1)
        rows_until = ones_where(row <= col)
        rows_until = jnp.concatenate([rows_until, rows_until, rows_until], axis=0)
        prior = jnp.zeros((1, HEADS), F32)
        for c in range(SPANS):
            logs = jnp.log2(dec_ref[:, c * SPAN : (c + 1) * SPAN])
            logs = jnp.concatenate(split3(logs), axis=1)
            sums = dot_nt(sums_of, logs)
            cum_ref[c] = sums[:SPAN]
            rows_ref[c] = dot(logs, rows_until)
            high, low = split2(jnp.exp2(sums[:SPAN] + prior))
            g_ref[c * SPAN : (c + 1) * SPAN, :] = jnp.concatenate([high, low], axis=1)
            prior = prior + sums[2 * SPAN : 2 * SPAN + 1]
            factor_ref[c] = jnp.concatenate(split2(jnp.exp2(sums)), axis=1)

    left = col < HEAD_DIM
    for u in range(TOGETHER):
        span = step * TOGETHER + u
        here = slice(u * SPAN, (u + 1) * SPAN)
        cum, cum_rows, factors = cum_ref[span], rows_ref[span], factor_ref[span]
        c_span, b_span = c_ref[here, :], b_ref[here, :]
        b_turned = b_span.T
        cross = jnp.where(col <= row, dot_nt(c_span, b_span), 0.0)
        for j in range(CHUNKS // 2):
            wide = slice(j * WIDE, (j + 1) * WIDE)
            spread_out = dot(factors, e_ref[:, wide])
            carry = carry_ref[:, wide]
            read = dot(c_span, carry.astype(BF16)) * spread_out[:SPAN]
            x_wide = x_ref[here, wide].astype(F32)
            parts = []
            for k in range(WIDE // 128):
                mixes = []
                for h in (first_head + j * 8 + 2 * k, first_head + j * 8 + 2 * k + 1):
                    spread = jnp.minimum(cum[:, h : h + 1] - cum_rows[h : h + 1, :], 0.0)
                    mixes.append((jnp.exp2(spread) * cross).astype(BF16))
                x_pair = x_ref[here, j * WIDE + k * 128 : j * WIDE + (k + 1) * 128]
                none = jnp.zeros_like(x_pair)
                x_both = jnp.concatenate(
                    [jnp.where(left, x_pair, none), jnp.where(left, none, x_pair)], axis=0
                )
                parts.append(dot(jnp.concatenate(mixes, axis=1), x_both))
            y = jnp.concatenate(parts, axis=1) + read + skip_ref[:, wide] * x_wide
            y_ref[here, wide] = y.astype(BF16)
            weighted = (x_wide * spread_out[SPAN : 2 * SPAN]).astype(BF16)
            carry_ref[:, wide] = spread_out[2 * SPAN : 2 * SPAN + 1] * carry + dot(b_turned, weighted)


def scan_kernel(in_ref, out_ref):
    carry = jnp.zeros((HALF, 128), F32)
    for k in range(PAIRS):
        out_ref[k] = carry.astype(BF16)
        decay = in_ref[k, HALF : HALF + 8, :].astype(F32)
        decay = decay[0:1] + decay[1:2]
        carry = decay * carry + in_ref[k, :HALF, :].astype(F32)


def score_kernel(
    base_ref, valid_ref, keep_ref, got_ref, c_ref, g_ref, left_any, right_any, z_any, gain_ref, head_ref,
    q0_ref, q1_ref, q2_ref, q3_ref, pair_ref, score_ref, paired_ref,
    e_ref, mean_ref, best_ref, enter_ref, q_ref, y_ref, z_ref, sems
):
    step = pl.program_id(0)

    def fetches(i):
        rows = pl.ds(i * BLOCK, BLOCK)
        return (
            pltpu.make_async_copy(left_any.at[rows, :], y_ref.at[0, i], sems.at[0, i]),
            pltpu.make_async_copy(right_any.at[rows, :], y_ref.at[1, i], sems.at[2, i]),
            pltpu.make_async_copy(z_any.at[rows, :], z_ref.at[i], sems.at[1, i]),
        )

    @pl.when(step == 0)
    def _():
        for i in range(TOKENS // BLOCK):
            for fetch in fetches(i):
                fetch.start()
        e_ref[...] = head_selector(2 * HEADS, 0, INNER)
        same = (iota((256, 256), 0) >> 6) == (iota((256, 256), 1) >> 6)
        mean_ref[...] = jnp.where(same, 1.0 / HEAD_DIM, 0.0).astype(BF16)
        for d in range(8):
            place = pl.multiple_of((base_ref[2] ^ d) * 16, 16)
            part = (q0_ref, q1_ref, q2_ref, q3_ref)[d // 2]
            for i in range(QTOK):
                q_ref[pl.ds(pl.multiple_of(i * QTOT + place, 16), 16), :] = part[d % 2, i]
        lower = base_ref[1] == 0
        for k in range(PAIRS):
            lanes = slice(k * 128, (k + 1) * 128)
            keep, got = keep_ref[k].astype(F32), got_ref[k].astype(F32)
            enter_ref[:HALF, lanes] = jnp.where(lower, keep, got).astype(BF16)
            enter_ref[HALF:, lanes] = jnp.where(lower, got, keep).astype(BF16)

    for fetch in fetches(step):
        fetch.wait()
    factors, c_part = g_ref[...], c_ref[...]
    embedded = jnp.zeros((BLOCK, EMB), F32)
    for j in range(2):
        wide = slice(j * INNER // 2, (j + 1) * INNER // 2)
        y = y_ref[j, step].astype(F32) + dot(factors, e_ref[:, wide]) * dot(c_part, enter_ref[:, wide])
        z_half = 0.5 * z_ref[step, :, wide].astype(F32)
        gated = y * (z_half + z_half * jnp.tanh(z_half))
        squares = (gated * gated).astype(BF16)
        means = jnp.concatenate(
            [dot(squares[:, k : k + 256], mean_ref[...]) for k in range(0, INNER // 2, 256)], axis=1
        )
        normed = (gated * lax.rsqrt(means + 1e-05) * gain_ref[:, wide]).astype(BF16)
        embedded = embedded + dot(normed, head_ref[wide, :])
    embedded = embedded * lax.rsqrt(jnp.sum(embedded * embedded, axis=1, keepdims=True) + 1e-06)
    for p in range(BLOCK // SPAN):
        passage = step * (BLOCK // SPAN) + p
        vectors = embedded[p * SPAN : (p + 1) * SPAN]
        kept = iota((SPAN, EMB), 0) < valid_ref[0, passage]
        vectors = jnp.where(kept, vectors, vectors[:1]).astype(BF16)
        for j in range(QTOK * QTOT // 1024):
            lanes = slice(j * 1024, (j + 1) * 1024)
            sims = dot_nt(vectors, q_ref[lanes, :])
            best_ref[pl.ds(passage, 1), lanes] = jnp.max(sims, axis=0, keepdims=True)

    @pl.when(step == TOKENS // BLOCK - 1)
    def _():
        total = best_ref[:, :QTOT]
        for i in range(1, QTOK):
            total = total + best_ref[:, i * QTOT : (i + 1) * QTOT]
        score_ref[...] = total
        matched = pair_ref[...] == base_ref[0] + iota((SPANS, QTOT), 0)
        paired = jnp.sum(jnp.where(matched, total, 0.0), axis=0, keepdims=True)
        paired_ref[...] = jnp.broadcast_to(paired, paired_ref.shape)


def whole(shape, space=None):
    kind = {} if space is None else {"memory_space": space}
    return pl.BlockSpec(shape, lambda i: (0,) * len(shape), **kind)


def params(mib):
    return pltpu.CompilerParams(
        dimension_semantics=("arbitrary",), vmem_limit_bytes=mib * 1024 * 1024
    )


def cost(flops, bytes_accessed, transcendentals=0):
    return pl.CostEstimate(
        flops=flops, bytes_accessed=bytes_accessed, transcendentals=transcendentals
    )


def device_states(core, decays, b, x):
    packed = jax.ShapeDtypeStruct((PAIRS, ROWS, 128), BF16)
    far = pl.BlockSpec(memory_space=pltpu.HBM)
    near = pl.BlockSpec(memory_space=pltpu.VMEM)
    return pl.pallas_call(
        states_kernel,
        in_specs=[pl.BlockSpec(memory_space=pltpu.SMEM), far, far, far],
        out_specs=[near, near],
        out_shape=[packed, packed],
        scratch_shapes=[
            pltpu.VMEM((HEADS, TOKENS), F32),
            pltpu.VMEM((TOKENS, STATE), BF16),
            pltpu.VMEM((CHUNKS, TOKENS, WIDE), BF16),
            pltpu.VMEM((TOKENS, 2 * HEADS), BF16),
            pltpu.VMEM((STATE, TOKENS), BF16),
            pltpu.SemaphoreType.DMA((CHUNKS + 2,)),
        ],
        compiler_params=pltpu.CompilerParams(vmem_limit_bytes=60 * 1024 * 1024),
        cost_estimate=cost(10**9, 5 * 10**6),
        name="device_states",
    )(core, decays, b, x)


def local_part(half, decays, b, c, x, skip):
    width = INNER // 2

    def tokens(columns, place=0):
        return pl.BlockSpec((TOGETHER * SPAN, columns), lambda i: (i, place))

    return pl.pallas_call(
        functools.partial(local_kernel, half * (HEADS // 2)),
        grid=(SPANS // TOGETHER,),
        in_specs=[
            whole((HEADS, TOKENS)),
            tokens(STATE),
            tokens(STATE),
            tokens(width, half),
            pl.BlockSpec((1, width), lambda i: (0, half)),
        ],
        out_specs=[tokens(width), whole((TOKENS, 2 * HEADS))],
        out_shape=[
            jax.ShapeDtypeStruct((TOKENS, width), BF16),
            jax.ShapeDtypeStruct((TOKENS, 2 * HEADS), BF16),
        ],
        scratch_shapes=[
            pltpu.VMEM((STATE, width), F32),
            pltpu.VMEM((2 * HEADS, width), BF16),
            pltpu.VMEM((SPANS, SPAN, HEADS), F32),
            pltpu.VMEM((SPANS, HEADS, SPAN), F32),
            pltpu.VMEM((SPANS, 2 * SPAN + 16, 2 * HEADS), BF16),
        ],
        compiler_params=params(60),
        cost_estimate=cost(4 * 10**9, 5 * 10**6, 2 * 10**6),
        name="local_part",
    )(decays, b, c, x, skip)


def scan_chips(states):
    return pl.pallas_call(
        scan_kernel,
        out_shape=jax.ShapeDtypeStruct((PAIRS, HALF, 128), BF16),
        compiler_params=pltpu.CompilerParams(vmem_limit_bytes=4 * 1024 * 1024),
        cost_estimate=cost(10**6, 600_000),
        name="scan_chips",
    )(states)


def scores(base, valid_len, keep, got, c, growth, left, right, z, gain, w_head, q, pair_ids):
    def tokens(width):
        return pl.BlockSpec((BLOCK, width), lambda i: (i, 0))

    smem = pl.BlockSpec(memory_space=pltpu.SMEM)
    far = pl.BlockSpec(memory_space=pltpu.HBM)
    half = whole((PAIRS, HALF, 128))
    everyone = 256
    return pl.pallas_call(
        score_kernel,
        grid=(TOKENS // BLOCK,),
        in_specs=[
            smem,
            smem,
            half,
            half,
            tokens(STATE),
            tokens(2 * HEADS),
            far,
            far,
            far,
            whole((1, INNER)),
            whole((INNER, EMB)),
            *[whole((2, QTOK, QTOT // 8, EMB))] * 4,
            whole((1, QTOT)),
        ],
        out_specs=[whole((SPANS, QTOT)), whole((everyone, QTOT))],
        out_shape=[
            jax.ShapeDtypeStruct((SPANS, QTOT), F32),
            jax.ShapeDtypeStruct((everyone, QTOT), F32),
        ],
        scratch_shapes=[
            pltpu.VMEM((2 * HEADS, INNER), BF16),
            pltpu.VMEM((256, 256), BF16),
            pltpu.VMEM((SPANS, QTOK * QTOT), F32),
            pltpu.VMEM((STATE, INNER), BF16),
            pltpu.VMEM((QTOK * QTOT, EMB), BF16),
            pltpu.VMEM((2, TOKENS // BLOCK, BLOCK, INNER // 2), BF16),
            pltpu.VMEM((TOKENS // BLOCK, BLOCK, INNER), BF16),
            pltpu.SemaphoreType.DMA((3, TOKENS // BLOCK)),
        ],
        compiler_params=params(60),
        cost_estimate=cost(6 * 10**9, 11 * 10**6, 2 * 10**6),
        name="scores",
    )(base, valid_len, keep, got, c, growth, left, right, z, gain, w_head, *q, pair_ids)


def swap_cores(v):
    return lax.ppermute(v, "core", [(0, 1), (1, 0)])


def decay_of(packed):
    return packed[:, HALF : HALF + 1].astype(F32) + packed[:, HALF + 1 : HALF + 2].astype(F32)


def on_device(
    x_inner, z_gate, b_proj, c_proj, decays, d_skip, norm_gain, w_head, queries, valid_len, pair_ids
):
    core = lax.axis_index("core")
    x, z, b, c, decay = x_inner[0], z_gate[0], b_proj[0], c_proj[0], decays[0]

    own, send = device_states(core.reshape(1), decay, b, x)
    got = swap_cores(send)
    lower = core == 0
    first = jnp.where(lower, own, got)
    second = jnp.where(lower, got, own)
    d_first, d_second = decay_of(first), decay_of(second)
    chip = d_second * first[:, :HALF].astype(F32) + second[:, :HALF].astype(F32)
    high, low = split2(d_first * d_second)
    fill = jnp.zeros((PAIRS, 14, 128), BF16)
    packed = jnp.concatenate([chip.astype(BF16), high, low, fill], axis=1)
    packed, decay, queries = lax.optimization_barrier((packed, decay, queries))
    by_pair = lax.all_to_all(packed, ("z", "y_lo"), 0, 0, tiled=True)

    wide = queries.astype(F32)
    q = (wide * lax.rsqrt(jnp.sum(wide * wide, axis=-1, keepdims=True) + 1e-06)).astype(BF16)
    q = lax.optimization_barrier(q.transpose(1, 0, 2))
    q_pair = jnp.stack([q, lax.ppermute(q, "y_hi", [(0, 1), (1, 0)])])
    document = lax.axis_index(("x", "y_hi"))
    place = lax.axis_index(("z", "y_lo", "core"))
    base = jnp.stack([(document * 32 + place) * SPANS, core, document])
    skip = jnp.repeat(d_skip, HEAD_DIM).reshape(1, INNER)
    left, growth = local_part(0, decay, b, c, x, skip)
    by_pair, left, growth, q_pair, base = lax.optimization_barrier(
        (by_pair, left, growth, q_pair, base)
    )
    prefix, q_pair, decay = lax.optimization_barrier((scan_chips(by_pair), q_pair, decay))
    entering = lax.all_to_all(prefix, ("z", "y_lo"), 0, 0, tiled=True)
    q_parts = [q_pair] + [
        lax.ppermute(q_pair, "x", [(i, i ^ d) for i in range(4)]) for d in range(1, 4)
    ]
    right, _ = local_part(1, decay, b, c, x, skip)
    entering, right = lax.optimization_barrier((entering, right))
    after = (
        d_first * entering.astype(F32) + first[:, :HALF].astype(F32)
    ).astype(BF16)
    keep = jnp.where(lower, entering, after)
    got = swap_cores(jnp.where(lower, after, entering))

    maxsim, paired = scores(
        base, valid_len, keep, got, c, growth, left, right, z, norm_gain.reshape(1, INNER), w_head,
        q_parts, pair_ids.reshape(1, QTOT),
    )
    everything = lax.all_to_all(paired, ("z", "y_lo", "core", "x", "y_hi"), 0, 0, tiled=True)
    return maxsim[None], jnp.sum(everything, axis=0)


def solution(mesh):
    cut = Mesh(mesh.devices.reshape(8, 2, 2, 4, 2), ("z", "y_lo", "core", "x", "y_hi"))
    seq, qry = ("z", "y_lo", "core"), ("x", "y_hi")
    return jax.shard_map(
        on_device,
        mesh=cut,
        in_specs=(
            P(qry, seq, None),
            P(qry, seq, None),
            P(qry, seq, None),
            P(qry, seq, None),
            P(qry, None, seq),
            P(),
            P(),
            P(),
            P(qry, None, None),
            P(qry, seq),
            P(),
        ),
        out_specs=(P(qry, seq, None), P()),
        check_vma=False,
    )
```
